32 devices in a mesh: visit: 8 (over y, x, core), strip: 4 (over z).
Axes of the slice: x: 2, y: 2, z: 4, core: 2. Of those that a mesh axis runs over, the one named last changes fastest.
Arguments:
- warped: float32 [8, 256, 2048], P('visit', None, 'strip'), may hold values from -8 to 8
- variance: float32 [8, 256, 2048], P('visit', None, 'strip'), may hold values from 1 to 16
- bad_pixels: int32 [8, 256, 2048], P('visit', None, 'strip'), may hold values 0 or 1
- row_offset: int32 [8], P('visit'), may hold values from 0 to 255
- visit_group: int32 [8], P('visit'), may hold values from 0 to 1
- coefficient: float32 [8, 9, 3], P('visit'), may hold values from -3 to 3
- basis_rows: float32 [9, 21], replicated, may hold values from -1.2 to 1.2
- basis_cols: float32 [9, 21], replicated, may hold values from -1.2 to 1.2
Outputs:
- flux_sum: float32 [2, 256, 2048], P(None, 'strip', 'visit')
- weight_sum: float32 [2, 256, 2048], P(None, 'strip', 'visit')
The draws below stay inside these ranges and needn't reach their ends.
All inputs are finite; a program needn't handle non-finite values. No bound on the sum of `bad_pixels` on one device may be relied on, other than what follows from the above.
Results may differ from the reference program's by a relative error of at most 0.0003.
Values sent between devices are 32-bit elements; how exact they have to be, the bound alone decides.
A program may use at most 64 MiB of HBM per device.

```python
import math
import jax
import jax.numpy as jnp
from jax import lax

W = 2048
KS = 21
NB = 9
NGROUP = 2
H = 256
VISITS = 8


def place_ends(drawn, stream_key, smallest, high):
    longest = drawn.shape.index(max(drawn.shape))
    spots = []
    for shift in (0, 1):
        where = [jax.random.randint(jax.random.fold_in(stream_key, axis), (), 0, length) for axis, length in enumerate(drawn.shape)]
        where[longest] = (where[longest] + shift) % drawn.shape[longest]
        spots.append(tuple(where))
    return drawn.at[spots[0]].set(smallest).at[spots[1]].set(high)


def shard_levels(rng, extent, shards, smallest, top_value):
    gain, own = 1.0, jax.random.fold_in(rng, 6)
    for axis_at, parts in shards:
        steps = jnp.exp(jax.random.uniform(jax.random.fold_in(own, axis_at), (parts,), jnp.float32, smallest / len(shards), top_value / len(shards)))
        gain = gain * jnp.repeat(steps, extent[axis_at] // parts).reshape([-1 if axis == axis_at else 1 for axis in range(len(extent))])
    return gain


def bell_draw(stream_key, dims, scale, limit, pieces=(), kind=jnp.bfloat16):
    result = scale * jax.random.normal(stream_key, dims, jnp.float32)
    if pieces:
        result = result * shard_levels(stream_key, dims, pieces, -0.22, 0.18)
    return jnp.clip(result, -limit, limit).astype(kind)


def setup_inputs(seed: int = 0) -> dict:
    splits = jax.random.split(jax.random.key(seed), 9)
    warped = bell_draw(splits[0], (VISITS, H, W), 1.0, 8.0, ((0, 8), (2, 4)), jnp.float32)
    variance = jnp.clip(jnp.exp(math.log(16.0) - 2.7725887 * jax.random.uniform(splits[1], (VISITS, H, W), jnp.float32) ** shard_levels(splits[1], (VISITS, H, W), ((0, 8), (2, 4)), -0.2, 0.2)), 1.0, 16.0)
    bad_pixels = place_ends((jax.random.randint(splits[2], (VISITS, H, W), 0, 8) < 1).astype(jnp.int32), jax.random.fold_in(splits[2], 1), 0, 1)
    row_offset = place_ends(jax.random.randint(splits[3], (VISITS,), 0, H), jax.random.fold_in(splits[3], 1), 0, H - 1).astype(jnp.int32)
    visit_group = place_ends(jax.random.randint(splits[4], (VISITS,), 0, NGROUP), jax.random.fold_in(splits[4], 1), 0, NGROUP - 1).astype(jnp.int32)
    coefficient = bell_draw(splits[5], (VISITS, NB, 3), 0.5, 3.0, ((0, 8),), jnp.float32)
    basis_rows = bell_draw(splits[6], (NB, KS), 0.2, 1.2, (), jnp.float32)
    basis_cols = bell_draw(splits[7], (NB, KS), 0.2, 1.2, (), jnp.float32)
    return {"warped": warped, "variance": variance, "bad_pixels": bad_pixels, "row_offset": row_offset, "visit_group": visit_group, "coefficient": coefficient, "basis_rows": basis_rows, "basis_cols": basis_cols}


def reference(warped, variance, bad_pixels, row_offset, visit_group, coefficient, basis_rows, basis_cols):
    radius = KS // 2
    height = warped.shape[1]
    width = warped.shape[2]
    highest = lax.Precision.HIGHEST
    xpos = 2.0 * jnp.arange(width, dtype=jnp.float32) / (width - 1) - 1.0
    ypos = 2.0 * jnp.arange(height, dtype=jnp.float32) / (height - 1) - 1.0
    kern_cols = basis_cols[:, None, None, :]
    kern_rows = basis_rows[:, None, :, None]

    def one_visit(carry, item):
        image, var_plane, flags, shift, group, coef = item
        weight = (1.0 - flags.astype(jnp.float32)) / var_plane
        index = (jnp.arange(height, dtype=jnp.int32) + shift.astype(jnp.int32)) % height
        aligned = jnp.take(image, index, axis=0)
        aligned_weight = jnp.take(weight, index, axis=0)
        colf = lax.conv_general_dilated(aligned[None, None], kern_cols, (1, 1), ((0, 0), (radius, radius)), precision=highest)
        filtered = lax.conv_general_dilated(colf, kern_rows, (1, 1), ((radius, radius), (0, 0)), feature_group_count=NB, precision=highest)[0]
        spatial = coef[:, 0][:, None, None] + coef[:, 1][:, None, None] * xpos[None, None, :] + coef[:, 2][:, None, None] * ypos[None, :, None]
        matched = jnp.sum(spatial * filtered, axis=0)
        member = (jnp.arange(NGROUP, dtype=jnp.int32) == group.astype(jnp.int32)).astype(jnp.float32)
        flux, wsum = carry
        flux = flux + member[:, None, None] * (aligned_weight * matched)[None]
        wsum = wsum + member[:, None, None] * aligned_weight[None]
        return (flux, wsum), None

    init = (jnp.zeros((NGROUP, height, width), jnp.float32), jnp.zeros((NGROUP, height, width), jnp.float32))
    (flux_sum, weight_sum), _ = lax.scan(one_visit, init, (warped, variance, bad_pixels, row_offset, visit_group, coefficient))
    return (flux_sum, weight_sum)
```

```python
import functools
import jax
import jax.numpy as jnp
from jax import lax
from jax.experimental import pallas as pl
from jax.experimental.pallas import tpu as pltpu
from jax.sharding import PartitionSpec as P

NGROUP = 2
LANES = 128
EDGE = 64
TAIL = 8
MESH = pl.DeviceIdType.MESH


def split(x):
    hi = x.astype(jnp.bfloat16)
    lo = (x - hi.astype(jnp.float32)).astype(jnp.bfloat16)
    return hi, lo


def dot3(ahi, alo, bhi, blo):
    dot = functools.partial(jnp.dot, preferred_element_type=jnp.float32)
    return dot(ahi, bhi) + dot(ahi, blo) + dot(alo, bhi)


def kernel(
    nvisit, nstrip,
    img, var, bad, off, grp, coef, brow, bcol,
    fout, wout,
    halo, w2, p2, ahi, alo, base, chi, clo, mhi, mlo, fhi, flo,
    wsend, fsend, wrecv, frecv,
    halo_send, halo_recv, wsend_sem, fsend_sem, wrecv_sem, frecv_sem,
):
    height, narrow = img.shape
    nb, ks = brow.shape
    radius = ks // 2
    rows = height // nstrip
    piece = fout.shape[2]
    per = narrow // piece
    block = mhi.shape[0] // 2
    depth = mhi.shape[1] // nb
    pad = (depth - block) // 2
    tall = fhi.shape[0] // nb
    cols = fhi.shape[1]
    v = lax.axis_index("visit")
    s = lax.axis_index("strip")
    home = v // per
    slot = v % per

    barrier = pltpu.get_barrier_semaphore()

    def greet(vv, ss):
        @pl.when(jnp.logical_not((vv == v) & (ss == s)))
        def _():
            pl.semaphore_signal(barrier, inc=1, device_id=(vv, ss), device_id_type=MESH)

    for q in range(nstrip):
        for p in range(per):
            greet(per * s + p, q)
    for u in range(nvisit):
        greet(u, home)

    @pl.when(s > 0)
    def _():
        pl.semaphore_signal(barrier, inc=1, device_id=(v, s - 1), device_id_type=MESH)

    @pl.when(s < nstrip - 1)
    def _():
        pl.semaphore_signal(barrier, inc=1, device_id=(v, s + 1), device_id_type=MESH)

    back = lax.rem(height - off[0], height)
    weight = (1.0 - bad[...].astype(jnp.float32)) / var[...]
    w2[...] = pltpu.roll(weight, back, 0)
    group = jnp.full((TAIL, piece), grp[0], jnp.int32).astype(jnp.float32)
    for q in range(nstrip):
        part = w2[q * rows : (q + 1) * rows, :]
        for p in range(per):
            wsend[q, p, 0:rows, :] = part[:, p * piece : (p + 1) * piece]
            wsend[q, p, rows : rows + TAIL, :] = group

    greeted = per * nstrip + nvisit - 2 * (home == s).astype(jnp.int32)
    greeted = greeted + (s > 0).astype(jnp.int32) + (s < nstrip - 1).astype(jnp.int32)
    pl.semaphore_wait(barrier, greeted)

    def to_left():
        return pltpu.make_async_remote_copy(
            src_ref=img.at[:, pl.ds(0, LANES)], dst_ref=halo.at[1],
            send_sem=halo_send.at[0], recv_sem=halo_recv.at[1],
            device_id=(v, s - 1), device_id_type=MESH,
        )

    def to_right():
        return pltpu.make_async_remote_copy(
            src_ref=img.at[:, pl.ds(narrow - LANES, LANES)], dst_ref=halo.at[0],
            send_sem=halo_send.at[1], recv_sem=halo_recv.at[0],
            device_id=(v, s + 1), device_id_type=MESH,
        )

    @pl.when(s > 0)
    def _():
        to_left().start()

    @pl.when(s < nstrip - 1)
    def _():
        to_right().start()

    def remote(send, recv, send_sem, recv_sem, q, p):
        return pltpu.make_async_remote_copy(
            src_ref=send.at[q, p], dst_ref=recv.at[v],
            send_sem=send_sem.at[q, p], recv_sem=recv_sem.at[v],
            device_id=(per * s + p, q), device_id_type=MESH,
        )

    def ship(send, recv, send_sem, recv_sem, q, p):
        mine = (per * s + p == v) & (s == q)

        @pl.when(mine)
        def _():
            pltpu.make_async_copy(send.at[q, p], recv.at[v], recv_sem.at[v]).start()

        @pl.when(jnp.logical_not(mine))
        def _():
            remote(send, recv, send_sem, recv_sem, q, p).start()

    for q in range(nstrip):
        for p in range(per):
            ship(wsend, wrecv, wsend_sem, wrecv_sem, q, p)

    lane = lax.broadcasted_iota(jnp.int32, (nb, 2 * LANES), 1)
    flipped = jnp.zeros((nb, 2 * LANES), jnp.float32)
    turn = (radius - EDGE - (ks - 1)) % (2 * LANES)
    skew = turn % 8
    for j in range(ks):
        flipped = jnp.where(lane == ks - 1 - j + skew, bcol[:, j : j + 1], flipped)
    base[0:nb, 0 : 2 * LANES] = flipped
    for k in range(nb):
        spread = jnp.broadcast_to(base[k : k + 1, 0 : 2 * LANES], (2 * LANES, 2 * LANES))
        spread = pltpu.roll(spread, turn - skew, 1, stride=1, stride_axis=0)
        hi, lo = split(spread[:, 0:LANES])
        chi[:, k * LANES : (k + 1) * LANES] = hi
        clo[:, k * LANES : (k + 1) * LANES] = lo

    base[...] = jnp.zeros_like(base)
    slide = (pad - radius) % depth
    start = slide % 8
    base[0:nb, start : start + ks] = brow[...]

    def row_table(first):
        r = lax.broadcasted_iota(jnp.int32, (block, depth), 0)
        c = lax.broadcasted_iota(jnp.int32, (block, depth), 1)
        inside = jnp.abs(c - pad - r) <= radius
        ri = lax.broadcasted_iota(jnp.int32, (block, LANES), 0) + first
        ypos = 2.0 * ri.astype(jnp.float32) / (height - 1) - 1.0
        for k in range(nb):
            spread = jnp.broadcast_to(base[k : k + 1, :], (block, depth))
            spread = pltpu.roll(spread, slide - start, 1, stride=1, stride_axis=0)
            spread = jnp.where(inside, spread, 0.0)
            lead = coef[k, 0] + coef[k, 2] * ypos
            lead = jnp.concatenate([lead] * (depth // LANES), axis=1)
            hi, lo = split(lead * spread)
            mhi[0:block, k * depth : (k + 1) * depth] = hi
            mlo[0:block, k * depth : (k + 1) * depth] = lo
            hi, lo = split(coef[k, 1] * spread)
            mhi[block : 2 * block, k * depth : (k + 1) * depth] = hi
            mlo[block : 2 * block, k * depth : (k + 1) * depth] = lo

    if height == block:
        row_table(0)

    p2[:, EDGE : EDGE + narrow] = img[...]

    @pl.when(s == 0)
    def _():
        halo[0] = jnp.zeros((height, LANES), jnp.float32)

    @pl.when(s == nstrip - 1)
    def _():
        halo[1] = jnp.zeros((height, LANES), jnp.float32)

    @pl.when(s > 0)
    def _():
        to_right().wait_recv()

    @pl.when(s < nstrip - 1)
    def _():
        to_left().wait_recv()

    p2[:, 0:EDGE] = halo[0, :, LANES - EDGE : LANES]
    p2[:, EDGE + narrow : 2 * EDGE + narrow] = halo[1, :, 0:EDGE]
    hi, lo = split(pltpu.roll(p2[...], back, 0))
    ahi[...] = hi
    alo[...] = lo

    if pad:
        fhi[...] = jnp.zeros_like(fhi)
        flo[...] = jnp.zeros_like(flo)
    for cb in range(narrow // cols):
        for b in range(cols // LANES):
            at = cb * cols + b * LANES
            f = dot3(
                ahi[:, at : at + 2 * LANES], alo[:, at : at + 2 * LANES], chi[...], clo[...]
            )
            for k in range(nb):
                hi, lo = split(f[:, k * LANES : (k + 1) * LANES])
                fhi[k * tall + pad : k * tall + pad + height, b * LANES : (b + 1) * LANES] = hi
                flo[k * tall + pad : k * tall + pad + height, b * LANES : (b + 1) * LANES] = lo
        ci = lax.broadcasted_iota(jnp.int32, (rows, cols), 1) + (s * narrow + cb * cols)
        xpos = 2.0 * ci.astype(jnp.float32) / (narrow * nstrip - 1) - 1.0
        for rb in range(height // block):
            if height != block:
                row_table(rb * block)
                res = jnp.zeros((2 * block, cols), jnp.float32)
                for k in range(nb):
                    span = pl.ds(k * tall + rb * block, depth)
                    cut = pl.ds(k * depth, depth)
                    res = res + dot3(mhi[:, cut], mlo[:, cut], fhi[span, :], flo[span, :])
            else:
                res = dot3(mhi[...], mlo[...], fhi[...], flo[...])
            for t in range(block // rows):
                q = rb * (block // rows) + t
                matched = (
                    res[t * rows : (t + 1) * rows]
                    + xpos * res[block + t * rows : block + (t + 1) * rows]
                )
                for i in range(cols // piece):
                    p = cb * (cols // piece) + i
                    fsend[q, p] = (
                        wsend[q, p, 0:rows, :] * matched[:, i * piece : (i + 1) * piece]
                    )
                    ship(fsend, frecv, fsend_sem, frecv_sem, q, p)

    def total(send, recv, send_sem, recv_sem, out):
        sums = [jnp.zeros((rows, piece), jnp.float32) for _ in range(NGROUP)]
        for u in range(nvisit):
            pltpu.make_async_copy(recv.at[u], recv.at[u], recv_sem.at[u]).wait()
            label = wrecv[u, rows : rows + 1, :]
            value = recv[u, 0:rows, :]
            for g in range(NGROUP):
                sums[g] = sums[g] + jnp.where(label == g, value, 0.0)
        for g in range(NGROUP):
            out[g] = sums[g]

    total(wsend, wrecv, wsend_sem, wrecv_sem, wout)
    total(fsend, frecv, fsend_sem, frecv_sem, fout)

    for send, recv, send_sem, recv_sem in (
        (wsend, wrecv, wsend_sem, wrecv_sem),
        (fsend, frecv, fsend_sem, frecv_sem),
    ):
        for q in range(nstrip):
            for p in range(per):
                @pl.when(jnp.logical_not((per * s + p == v) & (s == q)))
                def _():
                    remote(send, recv, send_sem, recv_sem, q, p).wait_send()

    @pl.when(s > 0)
    def _():
        to_left().wait_send()

    @pl.when(s < nstrip - 1)
    def _():
        to_right().wait_send()


def on_device(nvisit, nstrip, warped, variance, bad, offset, group, coefficient, brow, bcol):
    _, height, narrow = warped.shape
    nb, ks = brow.shape
    rows = height // nstrip
    piece = narrow * nstrip // nvisit
    per = narrow // piece
    block = min(height, 256)
    pad = 0 if block == height else LANES
    depth = block + 2 * pad
    tall = height + 2 * pad
    cols = min(narrow, 256)
    vmem = pl.BlockSpec(memory_space=pltpu.VMEM)
    smem = pl.BlockSpec(memory_space=pltpu.SMEM)
    f32, bf16 = jnp.float32, jnp.bfloat16
    dma = pltpu.SemaphoreType.DMA
    out = jax.ShapeDtypeStruct((NGROUP, rows, piece), f32)
    return pl.pallas_call(
        functools.partial(kernel, nvisit, nstrip),
        out_shape=(out, out),
        in_specs=[vmem, vmem, vmem, smem, smem, smem, vmem, vmem],
        out_specs=(vmem, vmem),
        scratch_shapes=[
            pltpu.VMEM((2, height, LANES), f32),
            pltpu.VMEM((height, narrow), f32),
            pltpu.VMEM((height, narrow + 2 * EDGE), f32),
            pltpu.VMEM((height, narrow + 2 * EDGE), bf16),
            pltpu.VMEM((height, narrow + 2 * EDGE), bf16),
            pltpu.VMEM((16, depth), f32),
            pltpu.VMEM((2 * LANES, nb * LANES), bf16),
            pltpu.VMEM((2 * LANES, nb * LANES), bf16),
            pltpu.VMEM((2 * block, nb * depth), bf16),
            pltpu.VMEM((2 * block, nb * depth), bf16),
            pltpu.VMEM((nb * tall, cols), bf16),
            pltpu.VMEM((nb * tall, cols), bf16),
            pltpu.VMEM((nstrip, per, rows + TAIL, piece), f32),
            pltpu.VMEM((nstrip, per, rows, piece), f32),
            pltpu.VMEM((nvisit, rows + TAIL, piece), f32),
            pltpu.VMEM((nvisit, rows, piece), f32),
            dma((2,)),
            dma((2,)),
            dma((nstrip, per)),
            dma((nstrip, per)),
            dma((nvisit,)),
            dma((nvisit,)),
        ],
        compiler_params=pltpu.CompilerParams(
            collective_id=0, has_side_effects=True, vmem_limit_bytes=52 * 2**20
        ),
    )(
        warped[0], variance[0], bad[0], offset, group, coefficient[0], brow, bcol
    )


def solution(mesh):
    return jax.shard_map(
        functools.partial(on_device, mesh.shape["visit"], mesh.shape["strip"]),
        mesh=mesh,
        in_specs=(
            P("visit", None, "strip"),
            P("visit", None, "strip"),
            P("visit", None, "strip"),
            P("visit"),
            P("visit"),
            P("visit", None, None),
            P(),
            P(),
        ),
        out_specs=(P(None, "strip", "visit"), P(None, "strip", "visit")),
        check_vma=False,
    )
```

```python
import functools
import jax
import jax.numpy as jnp
from jax import lax
from jax.experimental import pallas as pl
from jax.experimental.pallas import tpu as pltpu
from jax.sharding import PartitionSpec as P

NGROUP = 2
LANES = 128
EDGE = 64
TAIL = 8
MESH = pl.DeviceIdType.MESH


def split(x):
    hi = x.astype(jnp.bfloat16)
    lo = (x - hi.astype(jnp.float32)).astype(jnp.bfloat16)
    return hi, lo


def dot3(ahi, alo, bhi, blo):
    dot = functools.partial(jnp.dot, preferred_element_type=jnp.float32)
    return dot(ahi, bhi) + dot(ahi, blo) + dot(alo, bhi)


def kernel(
    nvisit, nstrip,
    img, var, bad, off, grp, coef, brow, bcol,
    fout, wout,
    varv, badv, hsend, hrecv, w2, p2, ahi, alo, base, chi, clo, mhi, mlo, fhi, flo,
    wsend, fsend, wrecv, frecv,
    load_sem, halo_send, halo_recv, wsend_sem, fsend_sem, wrecv_sem, frecv_sem,
):
    height, narrow = img.shape
    nb, ks = brow.shape
    radius = ks // 2
    rows = height // nstrip
    piece = fout.shape[2]
    per = narrow // piece
    block = mhi.shape[0] // 2
    depth = mhi.shape[1] // nb
    pad = (depth - block) // 2
    tall = fhi.shape[0] // nb
    cols = fhi.shape[1]
    v = lax.axis_index("visit")
    s = lax.axis_index("strip")
    home = v // per
    slot = v % per

    loads = [
        pltpu.make_async_copy(var, varv, load_sem.at[0]),
        pltpu.make_async_copy(bad, badv, load_sem.at[1]),
        pltpu.make_async_copy(img, p2.at[:, pl.ds(LANES, narrow)], load_sem.at[2]),
    ]
    for load in loads:
        load.start()

    barrier = pltpu.get_barrier_semaphore()

    def greet(vv, ss):
        @pl.when(jnp.logical_not((vv == v) & (ss == s)))
        def _():
            pl.semaphore_signal(barrier, inc=1, device_id=(vv, ss), device_id_type=MESH)

    for q in range(nstrip):
        for p in range(per):
            greet(per * s + p, q)
    for u in range(nvisit):
        greet(u, home)

    @pl.when(s > 0)
    def _():
        pl.semaphore_signal(barrier, inc=1, device_id=(v, s - 1), device_id_type=MESH)

    @pl.when(s < nstrip - 1)
    def _():
        pl.semaphore_signal(barrier, inc=1, device_id=(v, s + 1), device_id_type=MESH)

    back = lax.rem(height - off[0], height)
    loads[0].wait()
    loads[1].wait()
    weight = (1.0 - badv[...].astype(jnp.float32)) / varv[...]
    w2[...] = pltpu.roll(weight, back, 0)
    group = jnp.full((TAIL, piece), grp[0], jnp.int32).astype(jnp.float32)
    for q in range(nstrip):
        part = w2[q * rows : (q + 1) * rows, :]
        for p in range(per):
            wsend[q, p, 0:rows, :] = part[:, p * piece : (p + 1) * piece]
            wsend[q, p, rows : rows + TAIL, :] = group

    loads[2].wait()
    thin = LANES // 8
    short = height // 8
    for b in range(8):
        span = slice(b * short, (b + 1) * short)
        lanes = slice(b * thin, (b + 1) * thin)
        hsend[0, :, lanes] = p2[span, LANES : LANES + thin]
        hsend[1, :, lanes] = p2[span, LANES + narrow - thin : LANES + narrow]
    p2[:, 0:LANES] = jnp.zeros((height, LANES), jnp.float32)
    p2[:, LANES + narrow :] = jnp.zeros((height, LANES), jnp.float32)

    lane = lax.broadcasted_iota(jnp.int32, (nb, 2 * LANES), 1)
    flipped = jnp.zeros((nb, 2 * LANES), jnp.float32)
    turn = (radius - EDGE - (ks - 1)) % (2 * LANES)
    skew = turn % 8
    for j in range(ks):
        flipped = jnp.where(lane == ks - 1 - j + skew, bcol[:, j : j + 1], flipped)
    base[0:nb, 0 : 2 * LANES] = flipped
    for k in range(nb):
        spread = jnp.broadcast_to(base[k : k + 1, 0 : 2 * LANES], (2 * LANES, 2 * LANES))
        spread = pltpu.roll(spread, turn - skew, 1, stride=1, stride_axis=0)
        hi, lo = split(spread[:, 0:LANES])
        chi[:, k * LANES : (k + 1) * LANES] = hi
        clo[:, k * LANES : (k + 1) * LANES] = lo

    base[...] = jnp.zeros_like(base)
    slide = (pad - radius) % depth
    start = slide % 8
    base[0:nb, start : start + ks] = brow[...]

    def row_table(first):
        r = lax.broadcasted_iota(jnp.int32, (block, depth), 0)
        c = lax.broadcasted_iota(jnp.int32, (block, depth), 1)
        inside = jnp.abs(c - pad - r) <= radius
        ri = lax.broadcasted_iota(jnp.int32, (block, LANES), 0) + first
        ypos = 2.0 * ri.astype(jnp.float32) / (height - 1) - 1.0
        for k in range(nb):
            spread = jnp.broadcast_to(base[k : k + 1, :], (block, depth))
            spread = pltpu.roll(spread, slide - start, 1, stride=1, stride_axis=0)
            spread = jnp.where(inside, spread, 0.0)
            lead = coef[0, 0, k] + coef[2, 0, k] * ypos
            lead = jnp.concatenate([lead] * (depth // LANES), axis=1)
            hi, lo = split(lead * spread)
            mhi[0:block, k * depth : (k + 1) * depth] = hi
            mlo[0:block, k * depth : (k + 1) * depth] = lo
            hi, lo = split(coef[1, 0, k] * spread)
            mhi[block : 2 * block, k * depth : (k + 1) * depth] = hi
            mlo[block : 2 * block, k * depth : (k + 1) * depth] = lo

    if height == block:
        row_table(0)

    greeted = per * nstrip + nvisit - 2 * (home == s).astype(jnp.int32)
    greeted = greeted + (s > 0).astype(jnp.int32) + (s < nstrip - 1).astype(jnp.int32)
    pl.semaphore_wait(barrier, greeted)

    def to_left():
        return pltpu.make_async_remote_copy(
            src_ref=hsend.at[0], dst_ref=hrecv.at[1],
            send_sem=halo_send.at[0], recv_sem=halo_recv.at[1],
            device_id=(v, s - 1), device_id_type=MESH,
        )

    def to_right():
        return pltpu.make_async_remote_copy(
            src_ref=hsend.at[1], dst_ref=hrecv.at[0],
            send_sem=halo_send.at[1], recv_sem=halo_recv.at[0],
            device_id=(v, s + 1), device_id_type=MESH,
        )

    @pl.when(s > 0)
    def _():
        to_left().start()

    @pl.when(s < nstrip - 1)
    def _():
        to_right().start()

    def remote(send, recv, send_sem, recv_sem, q, p):
        return pltpu.make_async_remote_copy(
            src_ref=send.at[q, p], dst_ref=recv.at[v],
            send_sem=send_sem.at[q, p], recv_sem=recv_sem.at[v],
            device_id=(per * s + p, q), device_id_type=MESH,
        )

    def ship(send, recv, send_sem, recv_sem, q, p):
        mine = (per * s + p == v) & (s == q)

        @pl.when(mine)
        def _():
            pltpu.make_async_copy(send.at[q, p], recv.at[v], recv_sem.at[v]).start()

        @pl.when(jnp.logical_not(mine))
        def _():
            remote(send, recv, send_sem, recv_sem, q, p).start()

    for t in range(nstrip):
        for p in range(per):
            ship(wsend, wrecv, wsend_sem, wrecv_sem, (s + v // 2 + t) % nstrip, p)


    @pl.when(s > 0)
    def _():
        to_right().wait_recv()
        for b in range(8):
            span = slice(b * short, (b + 1) * short)
            p2[span, LANES - thin : LANES] = hrecv[0, :, b * thin : (b + 1) * thin]

    @pl.when(s < nstrip - 1)
    def _():
        to_left().wait_recv()
        for b in range(8):
            span = slice(b * short, (b + 1) * short)
            p2[span, LANES + narrow : LANES + narrow + thin] = hrecv[1, :, b * thin : (b + 1) * thin]

    aligned = pltpu.roll(p2[...], back, 0)
    hi, lo = split(aligned[:, LANES - EDGE : LANES + narrow + EDGE])
    ahi[...] = hi
    alo[...] = lo

    if pad:
        fhi[...] = jnp.zeros_like(fhi)
        flo[...] = jnp.zeros_like(flo)
    for cb in range(narrow // cols):
        for b in range(cols // LANES):
            at = cb * cols + b * LANES
            f = dot3(
                ahi[:, at : at + 2 * LANES], alo[:, at : at + 2 * LANES], chi[...], clo[...]
            )
            for k in range(nb):
                hi, lo = split(f[:, k * LANES : (k + 1) * LANES])
                fhi[k * tall + pad : k * tall + pad + height, b * LANES : (b + 1) * LANES] = hi
                flo[k * tall + pad : k * tall + pad + height, b * LANES : (b + 1) * LANES] = lo
        ci = lax.broadcasted_iota(jnp.int32, (rows, cols), 1) + (s * narrow + cb * cols)
        xpos = 2.0 * ci.astype(jnp.float32) / (narrow * nstrip - 1) - 1.0
        for rb in range(height // block):
            if height != block:
                row_table(rb * block)
                res = jnp.zeros((2 * block, cols), jnp.float32)
                for k in range(nb):
                    span = pl.ds(k * tall + rb * block, depth)
                    cut = pl.ds(k * depth, depth)
                    res = res + dot3(mhi[:, cut], mlo[:, cut], fhi[span, :], flo[span, :])
            else:
                res = dot3(mhi[...], mlo[...], fhi[...], flo[...])
            for t in range(block // rows):
                q = rb * (block // rows) + t
                matched = (
                    res[t * rows : (t + 1) * rows]
                    + xpos * res[block + t * rows : block + (t + 1) * rows]
                )
                for i in range(cols // piece):
                    p = cb * (cols // piece) + i
                    fsend[q, p] = (
                        wsend[q, p, 0:rows, :] * matched[:, i * piece : (i + 1) * piece]
                    )

        for t in range(nstrip):
            for i in range(cols // piece):
                p = cb * (cols // piece) + i
                ship(fsend, frecv, fsend_sem, frecv_sem, (s + v // 2 + t) % nstrip, p)

    def total(send, recv, send_sem, recv_sem, out):
        sums = [jnp.zeros((rows, piece), jnp.float32) for _ in range(NGROUP)]
        for u in range(nvisit):
            pltpu.make_async_copy(recv.at[u], recv.at[u], recv_sem.at[u]).wait()
            label = wrecv[u, rows : rows + 1, :]
            value = recv[u, 0:rows, :]
            for g in range(NGROUP):
                sums[g] = sums[g] + jnp.where(label == g, value, 0.0)
        for g in range(NGROUP):
            out[g] = sums[g]

    total(wsend, wrecv, wsend_sem, wrecv_sem, wout)
    total(fsend, frecv, fsend_sem, frecv_sem, fout)

    for send, recv, send_sem, recv_sem in (
        (wsend, wrecv, wsend_sem, wrecv_sem),
        (fsend, frecv, fsend_sem, frecv_sem),
    ):
        for q in range(nstrip):
            for p in range(per):
                @pl.when(jnp.logical_not((per * s + p == v) & (s == q)))
                def _():
                    remote(send, recv, send_sem, recv_sem, q, p).wait_send()

    @pl.when(s > 0)
    def _():
        to_left().wait_send()

    @pl.when(s < nstrip - 1)
    def _():
        to_right().wait_send()


def on_device(nvisit, nstrip, warped, variance, bad, offset, group, coefficient, brow, bcol):
    _, height, narrow = warped.shape
    nb, ks = brow.shape
    rows = height // nstrip
    piece = narrow * nstrip // nvisit
    per = narrow // piece
    block = min(height, 256)
    pad = 0 if block == height else LANES
    depth = block + 2 * pad
    tall = height + 2 * pad
    cols = min(narrow, 256)
    vmem = pl.BlockSpec(memory_space=pltpu.VMEM)
    hbm = pl.BlockSpec(memory_space=pltpu.HBM)
    smem = pl.BlockSpec(memory_space=pltpu.SMEM)
    f32, bf16 = jnp.float32, jnp.bfloat16
    dma = pltpu.SemaphoreType.DMA
    out = jax.ShapeDtypeStruct((NGROUP, rows, piece), f32)
    return pl.pallas_call(
        functools.partial(kernel, nvisit, nstrip),
        out_shape=(out, out),
        in_specs=[hbm, hbm, hbm, smem, smem, smem, vmem, vmem],
        out_specs=(vmem, vmem),
        scratch_shapes=[
            pltpu.VMEM((height, narrow), f32),
            pltpu.VMEM((height, narrow), jnp.int32),
            pltpu.VMEM((2, height // 8, LANES), f32),
            pltpu.VMEM((2, height // 8, LANES), f32),
            pltpu.VMEM((height, narrow), f32),
            pltpu.VMEM((height, narrow + 2 * LANES), f32),
            pltpu.VMEM((height, narrow + 2 * EDGE), bf16),
            pltpu.VMEM((height, narrow + 2 * EDGE), bf16),
            pltpu.VMEM((16, depth), f32),
            pltpu.VMEM((2 * LANES, nb * LANES), bf16),
            pltpu.VMEM((2 * LANES, nb * LANES), bf16),
            pltpu.VMEM((2 * block, nb * depth), bf16),
            pltpu.VMEM((2 * block, nb * depth), bf16),
            pltpu.VMEM((nb * tall, cols), bf16),
            pltpu.VMEM((nb * tall, cols), bf16),
            pltpu.VMEM((nstrip, per, rows + TAIL, piece), f32),
            pltpu.VMEM((nstrip, per, rows, piece), f32),
            pltpu.VMEM((nvisit, rows + TAIL, piece), f32),
            pltpu.VMEM((nvisit, rows, piece), f32),
            dma((3,)),
            dma((2,)),
            dma((2,)),
            dma((nstrip, per)),
            dma((nstrip, per)),
            dma((nvisit,)),
            dma((nvisit,)),
        ],
        compiler_params=pltpu.CompilerParams(
            collective_id=0, has_side_effects=True, vmem_limit_bytes=64 * 2**20 - 510 * 2**10
        ),
    )(
        warped[0], variance[0], bad[0], offset, group, jnp.transpose(coefficient, (2, 0, 1)), brow, bcol
    )


def solution(mesh):
    return jax.shard_map(
        functools.partial(on_device, mesh.shape["visit"], mesh.shape["strip"]),
        mesh=mesh,
        in_specs=(
            P("visit", None, "strip"),
            P("visit", None, "strip"),
            P("visit", None, "strip"),
            P("visit"),
            P("visit"),
            P("visit", None, None),
            P(),
            P(),
        ),
        out_specs=(P(None, "strip", "visit"), P(None, "strip", "visit")),
        check_vma=False,
    )
```

```python
import functools
import jax
import jax.numpy as jnp
from jax import lax
from jax.experimental import pallas as pl
from jax.experimental.pallas import tpu as pltpu
from jax.sharding import PartitionSpec as P

NGROUP = 2
LANES = 128
EDGE = 64
TAIL = 8
MESH = pl.DeviceIdType.MESH


def split(x):
    hi = x.astype(jnp.bfloat16)
    lo = (x - hi.astype(jnp.float32)).astype(jnp.bfloat16)
    return hi, lo


def dot3(ahi, alo, bhi, blo):
    dot = functools.partial(jnp.dot, preferred_element_type=jnp.float32)
    return dot(ahi, bhi) + dot(ahi, blo) + dot(alo, bhi)


def kernel(
    nvisit, nstrip,
    img, var, bad, off, grp, coef, brow, bcol,
    fout, wout,
    varv, badv, hsend, hrecv, w2, p2, ahi, alo, base, chi, clo, mhi, mlo, fhi, flo,
    wsend, fsend, wrecv, frecv,
    load_sem, halo_send, halo_recv, wsend_sem, fsend_sem, wrecv_sem, frecv_sem,
):
    height, narrow = img.shape
    nb, ks = brow.shape
    radius = ks // 2
    rows = height // nstrip
    piece = fout.shape[2]
    per = narrow // piece
    block = mhi.shape[0] // 2
    depth = mhi.shape[1] // nb
    pad = (depth - block) // 2
    tall = fhi.shape[0] // nb
    cols = fhi.shape[1]
    v = lax.axis_index("visit")
    s = lax.axis_index("strip")
    home = v // per
    slot = v % per

    loads = [
        pltpu.make_async_copy(var, varv, load_sem.at[0]),
        pltpu.make_async_copy(bad, badv, load_sem.at[1]),
        pltpu.make_async_copy(img, p2.at[:, pl.ds(LANES, narrow)], load_sem.at[2]),
    ]
    for load in loads:
        load.start()

    barrier = pltpu.get_barrier_semaphore()

    def greet(vv, ss):
        @pl.when(jnp.logical_not((vv == v) & (ss == s)))
        def _():
            pl.semaphore_signal(barrier, inc=1, device_id=(vv, ss), device_id_type=MESH)

    for q in range(nstrip):
        for p in range(per):
            greet(per * s + p, q)
    for u in range(nvisit):
        greet(u, home)

    @pl.when(s > 0)
    def _():
        pl.semaphore_signal(barrier, inc=1, device_id=(v, s - 1), device_id_type=MESH)

    @pl.when(s < nstrip - 1)
    def _():
        pl.semaphore_signal(barrier, inc=1, device_id=(v, s + 1), device_id_type=MESH)

    back = lax.rem(height - off[0], height)
    loads[0].wait()
    loads[1].wait()
    weight = (1.0 - badv[...].astype(jnp.float32)) / varv[...]
    w2[...] = pltpu.roll(weight, back, 0)
    group = jnp.full((TAIL, piece), grp[0], jnp.int32).astype(jnp.float32)
    for q in range(nstrip):
        part = w2[q * rows : (q + 1) * rows, :]
        for p in range(per):
            wsend[q, p, 0:rows, :] = part[:, p * piece : (p + 1) * piece]
            wsend[q, p, rows : rows + TAIL, :] = group

    loads[2].wait()
    thin = LANES // 8
    short = height // 8
    for b in range(8):
        span = slice(b * short, (b + 1) * short)
        lanes = slice(b * thin, (b + 1) * thin)
        hsend[0, :, lanes] = p2[span, LANES : LANES + thin]
        hsend[1, :, lanes] = p2[span, LANES + narrow - thin : LANES + narrow]
    p2[:, 0:LANES] = jnp.zeros((height, LANES), jnp.float32)
    p2[:, LANES + narrow :] = jnp.zeros((height, LANES), jnp.float32)

    lane = lax.broadcasted_iota(jnp.int32, (nb, 2 * LANES), 1)
    flipped = jnp.zeros((nb, 2 * LANES), jnp.float32)
    turn = (radius - EDGE - (ks - 1)) % (2 * LANES)
    skew = turn % 8
    for j in range(ks):
        flipped = jnp.where(lane == ks - 1 - j + skew, bcol[:, j : j + 1], flipped)
    base[0:nb, 0 : 2 * LANES] = flipped
    for k in range(nb):
        spread = jnp.broadcast_to(base[k : k + 1, 0 : 2 * LANES], (2 * LANES, 2 * LANES))
        spread = pltpu.roll(spread, turn - skew, 1, stride=1, stride_axis=0)
        hi, lo = split(spread[:, 0:LANES])
        chi[:, k * LANES : (k + 1) * LANES] = hi
        clo[:, k * LANES : (k + 1) * LANES] = lo

    base[...] = jnp.zeros_like(base)
    slide = (pad - radius) % depth
    start = slide % 8
    base[0:nb, start : start + ks] = brow[...]

    def row_table(first):
        r = lax.broadcasted_iota(jnp.int32, (block, depth), 0)
        c = lax.broadcasted_iota(jnp.int32, (block, depth), 1)
        inside = jnp.abs(c - pad - r) <= radius
        ri = lax.broadcasted_iota(jnp.int32, (block, LANES), 0) + first
        ypos = 2.0 * ri.astype(jnp.float32) / (height - 1) - 1.0
        for k in range(nb):
            spread = jnp.broadcast_to(base[k : k + 1, :], (block, depth))
            spread = pltpu.roll(spread, slide - start, 1, stride=1, stride_axis=0)
            spread = jnp.where(inside, spread, 0.0)
            lead = coef[0, 0, k] + coef[2, 0, k] * ypos
            lead = jnp.concatenate([lead] * (depth // LANES), axis=1)
            hi, lo = split(lead * spread)
            mhi[0:block, k * depth : (k + 1) * depth] = hi
            mlo[0:block, k * depth : (k + 1) * depth] = lo
            hi, lo = split(coef[1, 0, k] * spread)
            mhi[block : 2 * block, k * depth : (k + 1) * depth] = hi
            mlo[block : 2 * block, k * depth : (k + 1) * depth] = lo

    if height == block:
        row_table(0)

    greeted = per * nstrip + nvisit - 2 * (home == s).astype(jnp.int32)
    greeted = greeted + (s > 0).astype(jnp.int32) + (s < nstrip - 1).astype(jnp.int32)
    pl.semaphore_wait(barrier, greeted)

    def to_left():
        return pltpu.make_async_remote_copy(
            src_ref=hsend.at[0], dst_ref=hrecv.at[1],
            send_sem=halo_send.at[0], recv_sem=halo_recv.at[1],
            device_id=(v, s - 1), device_id_type=MESH,
        )

    def to_right():
        return pltpu.make_async_remote_copy(
            src_ref=hsend.at[1], dst_ref=hrecv.at[0],
            send_sem=halo_send.at[1], recv_sem=halo_recv.at[0],
            device_id=(v, s + 1), device_id_type=MESH,
        )

    @pl.when(s > 0)
    def _():
        to_left().start()

    @pl.when(s < nstrip - 1)
    def _():
        to_right().start()

    def remote(send, recv, send_sem, recv_sem, q, p):
        return pltpu.make_async_remote_copy(
            src_ref=send.at[q, p], dst_ref=recv.at[v],
            send_sem=send_sem.at[q, p], recv_sem=recv_sem.at[v],
            device_id=(per * s + p, q), device_id_type=MESH,
        )

    def ship(send, recv, send_sem, recv_sem, q, p):
        mine = (per * s + p == v) & (s == q)

        @pl.when(mine)
        def _():
            pltpu.make_async_copy(send.at[q, p], recv.at[v], recv_sem.at[v]).start()

        @pl.when(jnp.logical_not(mine))
        def _():
            remote(send, recv, send_sem, recv_sem, q, p).start()

    for t in range(nstrip):
        for p in range(per):
            ship(wsend, wrecv, wsend_sem, wrecv_sem, (s + nstrip // 2 + t) % nstrip, p)


    @pl.when(s > 0)
    def _():
        to_right().wait_recv()
        for b in range(8):
            span = slice(b * short, (b + 1) * short)
            p2[span, LANES - thin : LANES] = hrecv[0, :, b * thin : (b + 1) * thin]

    @pl.when(s < nstrip - 1)
    def _():
        to_left().wait_recv()
        for b in range(8):
            span = slice(b * short, (b + 1) * short)
            p2[span, LANES + narrow : LANES + narrow + thin] = hrecv[1, :, b * thin : (b + 1) * thin]

    aligned = pltpu.roll(p2[...], back, 0)
    hi, lo = split(aligned[:, LANES - EDGE : LANES + narrow + EDGE])
    ahi[...] = hi
    alo[...] = lo

    if pad:
        fhi[...] = jnp.zeros_like(fhi)
        flo[...] = jnp.zeros_like(flo)
    for cb in range(narrow // cols):
        for b in range(cols // LANES):
            at = cb * cols + b * LANES
            f = dot3(
                ahi[:, at : at + 2 * LANES], alo[:, at : at + 2 * LANES], chi[...], clo[...]
            )
            for k in range(nb):
                hi, lo = split(f[:, k * LANES : (k + 1) * LANES])
                fhi[k * tall + pad : k * tall + pad + height, b * LANES : (b + 1) * LANES] = hi
                flo[k * tall + pad : k * tall + pad + height, b * LANES : (b + 1) * LANES] = lo
        ci = lax.broadcasted_iota(jnp.int32, (rows, cols), 1) + (s * narrow + cb * cols)
        xpos = 2.0 * ci.astype(jnp.float32) / (narrow * nstrip - 1) - 1.0
        for rb in range(height // block):
            if height != block:
                row_table(rb * block)
                res = jnp.zeros((2 * block, cols), jnp.float32)
                for k in range(nb):
                    span = pl.ds(k * tall + rb * block, depth)
                    cut = pl.ds(k * depth, depth)
                    res = res + dot3(mhi[:, cut], mlo[:, cut], fhi[span, :], flo[span, :])
            else:
                res = dot3(mhi[...], mlo[...], fhi[...], flo[...])
            for t in range(block // rows):
                q = rb * (block // rows) + t
                matched = (
                    res[t * rows : (t + 1) * rows]
                    + xpos * res[block + t * rows : block + (t + 1) * rows]
                )
                for i in range(cols // piece):
                    p = cb * (cols // piece) + i
                    fsend[q, p] = (
                        wsend[q, p, 0:rows, :] * matched[:, i * piece : (i + 1) * piece]
                    )

        for t in range(nstrip):
            for i in range(cols // piece):
                p = cb * (cols // piece) + i
                ship(fsend, frecv, fsend_sem, frecv_sem, (s + nstrip // 2 + t) % nstrip, p)

    def total(send, recv, send_sem, recv_sem, out):
        sums = [jnp.zeros((rows, piece), jnp.float32) for _ in range(NGROUP)]
        for u in range(nvisit):
            pltpu.make_async_copy(recv.at[u], recv.at[u], recv_sem.at[u]).wait()
            label = wrecv[u, rows : rows + 1, :]
            value = recv[u, 0:rows, :]
            for g in range(NGROUP):
                sums[g] = sums[g] + jnp.where(label == g, value, 0.0)
        for g in range(NGROUP):
            out[g] = sums[g]

    total(wsend, wrecv, wsend_sem, wrecv_sem, wout)
    total(fsend, frecv, fsend_sem, frecv_sem, fout)

    for send, recv, send_sem, recv_sem in (
        (wsend, wrecv, wsend_sem, wrecv_sem),
        (fsend, frecv, fsend_sem, frecv_sem),
    ):
        for q in range(nstrip):
            for p in range(per):
                @pl.when(jnp.logical_not((per * s + p == v) & (s == q)))
                def _():
                    remote(send, recv, send_sem, recv_sem, q, p).wait_send()

    @pl.when(s > 0)
    def _():
        to_left().wait_send()

    @pl.when(s < nstrip - 1)
    def _():
        to_right().wait_send()


def on_device(nvisit, nstrip, warped, variance, bad, offset, group, coefficient, brow, bcol):
    _, height, narrow = warped.shape
    nb, ks = brow.shape
    rows = height // nstrip
    piece = narrow * nstrip // nvisit
    per = narrow // piece
    block = min(height, 256)
    pad = 0 if block == height else LANES
    depth = block + 2 * pad
    tall = height + 2 * pad
    cols = min(narrow, 256)
    vmem = pl.BlockSpec(memory_space=pltpu.VMEM)
    hbm = pl.BlockSpec(memory_space=pltpu.HBM)
    smem = pl.BlockSpec(memory_space=pltpu.SMEM)
    f32, bf16 = jnp.float32, jnp.bfloat16
    dma = pltpu.SemaphoreType.DMA
    out = jax.ShapeDtypeStruct((NGROUP, rows, piece), f32)
    return pl.pallas_call(
        functools.partial(kernel, nvisit, nstrip),
        out_shape=(out, out),
        in_specs=[hbm, hbm, hbm, smem, smem, smem, vmem, vmem],
        out_specs=(vmem, vmem),
        scratch_shapes=[
            pltpu.VMEM((height, narrow), f32),
            pltpu.VMEM((height, narrow), jnp.int32),
            pltpu.VMEM((2, height // 8, LANES), f32),
            pltpu.VMEM((2, height // 8, LANES), f32),
            pltpu.VMEM((height, narrow), f32),
            pltpu.VMEM((height, narrow + 2 * LANES), f32),
            pltpu.VMEM((height, narrow + 2 * EDGE), bf16),
            pltpu.VMEM((height, narrow + 2 * EDGE), bf16),
            pltpu.VMEM((16, depth), f32),
            pltpu.VMEM((2 * LANES, nb * LANES), bf16),
            pltpu.VMEM((2 * LANES, nb * LANES), bf16),
            pltpu.VMEM((2 * block, nb * depth), bf16),
            pltpu.VMEM((2 * block, nb * depth), bf16),
            pltpu.VMEM((nb * tall, cols), bf16),
            pltpu.VMEM((nb * tall, cols), bf16),
            pltpu.VMEM((nstrip, per, rows + TAIL, piece), f32),
            pltpu.VMEM((nstrip, per, rows, piece), f32),
            pltpu.VMEM((nvisit, rows + TAIL, piece), f32),
            pltpu.VMEM((nvisit, rows, piece), f32),
            dma((3,)),
            dma((2,)),
            dma((2,)),
            dma((nstrip, per)),
            dma((nstrip, per)),
            dma((nvisit,)),
            dma((nvisit,)),
        ],
        compiler_params=pltpu.CompilerParams(
            collective_id=0, has_side_effects=True, vmem_limit_bytes=64 * 2**20 - 510 * 2**10
        ),
    )(
        warped[0], variance[0], bad[0], offset, group, jnp.transpose(coefficient, (2, 0, 1)), brow, bcol
    )


def solution(mesh):
    return jax.shard_map(
        functools.partial(on_device, mesh.shape["visit"], mesh.shape["strip"]),
        mesh=mesh,
        in_specs=(
            P("visit", None, "strip"),
            P("visit", None, "strip"),
            P("visit", None, "strip"),
            P("visit"),
            P("visit"),
            P("visit", None, None),
            P(),
            P(),
        ),
        out_specs=(P(None, "strip", "visit"), P(None, "strip", "visit")),
        check_vma=False,
    )
```
